512 devices in a mesh: dp: 8 (over x, core), row: 4 (over z_lo), col: 16 (over z_hi, y).
Axes of the slice: x: 4, y: 8, z: 8 (z_hi: 2, z_lo: 4; z = z_hi * 4 + z_lo), core: 2. Of those that a mesh axis runs over, the one named last changes fastest.
Arguments:
- activations: bfloat16 [2048, 7424], P('col', ('dp', 'row')), may hold values from -6 to 6
- upstream: bfloat16 [2048, 29696], P(('dp', 'row'), 'col'), may hold values from -0.25 to 0.25
- weight: bfloat16 [7424, 29696], P(('dp', 'row'), 'col'), may hold values from -1.5 to 1.5
- bin_fill: int32 [32], P(('dp', 'row')), may hold values from 16 to 64, as said below
Outputs:
- d_input: bfloat16 [2048, 7424], P('col', ('dp', 'row'))
- d_weight: bfloat16 [7424, 29696], P(('dp', 'row'), 'col')
The draws below stay inside these ranges and needn't reach their ends.
Inputs may be any that keep to these rules, and one draw needn't show every extreme that they name: `bin_fill`: in every draw some bin is full, with 64 tokens, and some bin holds 16 tokens.
All inputs are finite; a program needn't handle non-finite values.
Results may differ from the reference program's by a relative error of at most 0.001.
Values may be sent and summed in bfloat16 or wider, within the bound.
No kernel may reach another device: no remote copies, remote signals or barrier semaphores. Data moves between devices by JAX's collectives and lax.ppermute only.
A program may use at most 64 MiB of HBM per device.

```python
import jax
import jax.numpy as jnp

D = 7424
FF = 29696
TOKENS = 2048
BIN_LEN = 64
BINS = 32


def draw_bin_fill(key, part):
    key = jax.random.fold_in(key, 11)
    first_key, second_key = jax.random.split(key)
    lowest = max(BIN_LEN // 4, 1)
    fills = jax.random.randint(first_key, (BINS,), lowest, BIN_LEN + 1)
    chosen = jax.random.randint(second_key, (), 0, BINS)
    places = jnp.arange(BINS, dtype=jnp.int32)
    fills = jnp.where(places == chosen, BIN_LEN, fills)
    fills = jnp.where(places == (chosen + 1) % BINS, lowest, fills)
    return fills.astype(jnp.int32)


def strengthened(array, key, source, target, parts, factor):
    def block_of(dim):
        return (jnp.arange(array.shape[dim]) // (array.shape[dim] // parts)).reshape((-1,) + (1,) * (array.ndim - 1 - dim))

    near = jax.random.permutation(key, parts)[block_of(target)]
    other_side = (block_of(target) + parts // 2) % parts
    return jnp.where((block_of(source) == near) | (block_of(source) == other_side), factor * array, array)


def block_levels(own_key, dims, pieces, low, top_value):
    def one(position, shards_of):
        steps = jax.random.uniform(jax.random.fold_in(jax.random.fold_in(own_key, 6), position), (shards_of,), jnp.float32, low / len(pieces), top_value / len(pieces))
        return jnp.repeat(jnp.exp(steps), dims[position] // shards_of).reshape((-1,) + (1,) * (len(dims) - position - 1))

    factor_of = one(*pieces[0])
    for cut in pieces[1:]:
        factor_of = factor_of * one(*cut)
    return factor_of


def scatter_about(own_key, extent, spread, limit, cuts=(), held_as=jnp.bfloat16):
    array = jax.random.normal(own_key, extent, jnp.float32) * spread
    if len(cuts) > 0:
        array = block_levels(own_key, extent, cuts, -0.22, 0.18) * array
    return jnp.clip(array, min=-limit, max=limit).astype(held_as)


def bell_draw_with(own_key, dims, deviation, reach, cuts, heavy, held_as=jnp.bfloat16):
    entries = deviation * jax.random.normal(own_key, dims, jnp.float32)
    if cuts:
        entries = entries * block_levels(own_key, dims, cuts, -0.22, 0.18)
    return jnp.clip(strengthened(entries, jax.random.fold_in(own_key, 3), *heavy), -reach, reach).astype(held_as)


def setup_inputs(seed: int = 0) -> dict:
    streams_of = jax.random.split(jax.random.key(seed), 5)
    activations = scatter_about(streams_of[0], (TOKENS, D), 1.0, 6.0, ((0, 16), (1, 32)))
    upstream = bell_draw_with(streams_of[1], (TOKENS, FF), (TOKENS ** -0.5), 0.25, ((0, 32), (1, 16)), (1, 0, 32, 2.75))
    weight = scatter_about(streams_of[2], (D, FF), (max(FF // TOKENS, 1)) ** -0.5, 1.5, ((0, 32), (1, 16)))
    bin_fill = draw_bin_fill(jax.random.fold_in(streams_of[4], 71), 0)
    return {"activations": activations, "upstream": upstream, "weight": weight, "bin_fill": bin_fill}


def reference(activations, upstream, weight, bin_fill):
    slot_index = jnp.arange(TOKENS, dtype=jnp.int32) % BIN_LEN
    owner_bin = jnp.arange(TOKENS, dtype=jnp.int32) // BIN_LEN
    live_rows = slot_index < bin_fill[owner_bin]
    masked = jnp.where(live_rows[:, None], upstream, jnp.zeros_like(upstream))
    d_input = jnp.dot(masked, weight.T, preferred_element_type=jnp.float32).astype(jnp.bfloat16)
    d_weight = jnp.dot(activations.T, masked, preferred_element_type=jnp.float32).astype(jnp.bfloat16)
    return d_input, d_weight
```

```python
import functools

import jax
import jax.numpy as jnp
from jax import lax
from jax.experimental import pallas as pl
from jax.experimental.pallas import tpu as pltpu
from jax.sharding import PartitionSpec as P

CHUNKS = 2
X, CORES, ROWS, FAR, NEAR = 4, 2, 4, 2, 8


def over_x(shift):
    return [(x * CORES + k, (x + shift) % X * CORES + k) for x in range(X) for k in range(CORES)]


def over_core():
    return [(i, i ^ 1) for i in range(X * CORES)]


def over_row(flip):
    return [(i, i ^ flip) for i in range(ROWS)]


def over_near(shift):
    return [(f * NEAR + y, f * NEAR + (y + shift) % NEAR) for f in range(FAR) for y in range(NEAR)]


def over_far():
    return [(i, (i + NEAR) % (FAR * NEAR)) for i in range(FAR * NEAR)]


def partial_kernel(live, places, *refs):
    (where_ref, pieces, weight_ref, tokens, sums, sems) = (
        refs[0], refs[1:1 + len(places)], refs[1 + len(places)], refs[2 + len(places)], refs[3 + len(places):-1], refs[-1])
    copies = []
    n = 0
    for piece, blocks in zip(pieces, places):
        for place in range(blocks):
            copies.append(pltpu.make_async_copy(
                piece.at[pl.ds(place * live, live)],
                tokens.at[pl.ds(pl.multiple_of(where_ref[n] * live, live), live)],
                sems.at[n]))
            n += 1
    for copy in copies:
        copy.start()
    for copy in copies:
        copy.wait()
    width = sums[0].shape[1]
    group = max(256 // width, 1)
    for first in range(0, NEAR, group):
        result = lax.dot_general(
            weight_ref[...], tokens[first * width:(first + group) * width],
            (((1,), (1,)), ((), ())), preferred_element_type=jnp.float32)
        for j in range(group):
            sums[first + j][...] = result[:, j * width:(j + 1) * width]


def partials(pieces, places, where, weight, live):
    features, hidden = weight.shape
    width = 4 * live
    rows = NEAR * width
    out_shape = [jax.ShapeDtypeStruct((rows, hidden), jnp.bfloat16)]
    out_shape += [jax.ShapeDtypeStruct((features, width), jnp.float32)] * NEAR
    vmem = pl.BlockSpec(memory_space=pltpu.VMEM)
    return pl.pallas_call(
        functools.partial(partial_kernel, live, places),
        out_shape=out_shape,
        in_specs=[pl.BlockSpec(memory_space=pltpu.SMEM)] + [pl.BlockSpec(memory_space=pl.ANY)] * len(pieces) + [vmem],
        out_specs=[vmem] * (1 + NEAR),
        scratch_shapes=[pltpu.SemaphoreType.DMA((sum(places),))],
        compiler_params=pltpu.CompilerParams(vmem_limit_bytes=40 << 20),
        cost_estimate=pl.CostEstimate(
            flops=2 * rows * hidden * features, bytes_accessed=4 * rows * hidden, transcendentals=0),
    )(where, *pieces, weight)


def weight_grad_kernel(chunks, *refs):
    inputs, tokens, out, held = refs[:NEAR], refs[NEAR:NEAR + chunks], refs[-2], refs[-1]
    features, width = out.shape[0], inputs[0].shape[1]
    for k in range(chunks):
        for y in range(NEAR):
            first = (k * NEAR + y) * width
            held[:, first:first + width] = inputs[y][k * features:(k + 1) * features, :]
    step = 128
    hidden = out.shape[1]
    rows = NEAR * width
    for first in range(0, hidden, 256):
        last = min(first + 256, hidden)
        total = None
        for k in range(chunks):
            part = lax.dot_general(
                held[:, k * rows:(k + 1) * rows], tokens[k][:, first:last],
                (((1,), (0,)), ((), ())), preferred_element_type=jnp.float32)
            total = part if total is None else total + part
        out[:, first:last] = total.astype(out.dtype)


def weight_grad(inputs, tokens):
    chunks = len(tokens)
    features = inputs[0].shape[0] // chunks
    rows, hidden = tokens[0].shape
    vmem = pl.BlockSpec(memory_space=pltpu.VMEM)
    return pl.pallas_call(
        functools.partial(weight_grad_kernel, chunks),
        out_shape=jax.ShapeDtypeStruct((features, hidden), jnp.bfloat16),
        in_specs=[vmem] * (NEAR + chunks),
        out_specs=vmem,
        scratch_shapes=[pltpu.VMEM((features, chunks * rows), jnp.bfloat16)],
        compiler_params=pltpu.CompilerParams(vmem_limit_bytes=40 << 20),
        cost_estimate=pl.CostEstimate(
            flops=2 * chunks * rows * hidden * features, bytes_accessed=2 * chunks * rows * hidden, transcendentals=0),
    )(*inputs, *tokens)


def on_device(activations, upstream, weight, bin_fill):
    bin_len, hidden = upstream.shape
    features = activations.shape[1]
    live = bin_len // CHUNKS
    dp, row, col = lax.axis_index("dp"), lax.axis_index("row"), lax.axis_index("col")
    x, core = dp // CORES, dp % CORES
    far, near = col // NEAR, col % NEAR

    slot_index = jnp.arange(bin_len, dtype=jnp.int32)
    masked = jnp.where((slot_index < bin_fill[0])[:, None], upstream, jnp.zeros_like(upstream))

    mine = activations.T.reshape(features, 2, CHUNKS, live)
    mine = mine.transpose(2, 0, 1, 3).reshape(CHUNKS * features, 2 * live)
    other = lax.ppermute(mine, "col", over_far())
    mine = jnp.where(far == 0, jnp.concatenate([mine, other], 1), jnp.concatenate([other, mine], 1))
    inputs = [None] * NEAR
    inputs[0] = mine
    up = down = mine
    for step in range(1, NEAR // 2 + 1):
        up = lax.ppermute(up, "col", over_near(1))
        inputs[-step % NEAR] = up
        if step < NEAR // 2:
            down = lax.ppermute(down, "col", over_near(-1))
            inputs[step] = down

    def place(x_of, core_of, flip):
        row_of = row ^ flip
        near_of = (x_of % 2 * 2 + core_of) * 2 + row_of // 2
        return ((near_of - near) % NEAR * 2 + x_of // 2) * 2 + row_of % 2

    tokens, sums = [], []
    for k in range(CHUNKS):
        block = masked[k * live:(k + 1) * live]
        four = jnp.concatenate([block] + [lax.ppermute(block, "row", over_row(flip)) for flip in (1, 2, 3)], 0)
        left = lax.ppermute(four, "dp", over_x(1))
        right = lax.ppermute(four, "dp", over_x(-1))
        across = [lax.ppermute(left[:2 * live], "dp", over_x(1)), lax.ppermute(right[2 * live:], "dp", over_x(-1))]
        own = [four, left, right] + across
        pieces = own + [lax.ppermute(piece, "dp", over_core()) for piece in own]
        places, where = [], []
        for core_of in (core, 1 - core):
            for x_of, flips in ((x, (0, 1, 2, 3)), ((x + 3) % X, (0, 1, 2, 3)), ((x + 1) % X, (0, 1, 2, 3)), ((x + 2) % X, (0, 1)), ((x + 2) % X, (2, 3))):
                places.append(len(flips))
                where += [place(x_of, core_of, flip) for flip in flips]
        held, *parts = partials(pieces, places, jnp.stack(where).astype(jnp.int32), weight, live)
        tokens.append(held)
        up, down = parts[4], parts[5]
        for step in range(1, 5):
            up = lax.ppermute(up, "col", over_near(1)) + parts[4 - step]
            if step < 4:
                down = lax.ppermute(down, "col", over_near(-1))
                if step < 3:
                    down = down + parts[5 + step]
        sums.append(up + down)

    half = 2 * live
    keep = jnp.concatenate([jnp.where(far == 0, s[:, :half], s[:, half:]) for s in sums], 1)
    send = jnp.concatenate([jnp.where(far == 0, s[:, half:], s[:, :half]) for s in sums], 1)
    total = keep + lax.ppermute(send, "col", over_far())
    d_input = total.reshape(features, CHUNKS, 2, live).transpose(0, 2, 1, 3).reshape(features, 2 * bin_len)
    d_input = d_input.T.astype(jnp.bfloat16)
    return d_input, weight_grad(inputs, tokens)


def solution(mesh):
    in_specs = (
        P("col", ("dp", "row")),
        P(("dp", "row"), "col"),
        P(("dp", "row"), "col"),
        P(("dp", "row")),
    )
    out_specs = (P("col", ("dp", "row")), P(("dp", "row"), "col"))
    return jax.shard_map(
        on_device, mesh=mesh, in_specs=in_specs, out_specs=out_specs, check_vma=False
    )
```

```python
import functools

import jax
import jax.numpy as jnp
from jax import lax
from jax.experimental import pallas as pl
from jax.experimental.pallas import tpu as pltpu
from jax.sharding import Mesh
from jax.sharding import PartitionSpec as P

CHUNKS = 2
X, CORES, ROWS, FAR, NEAR = 4, 2, 4, 2, 8
BLOCKS = 4
VMEM = pl.BlockSpec(memory_space=pltpu.VMEM)


def flips(size, flip):
    return [(i, i ^ flip) for i in range(size)]


def partial_kernel(live, packed, where_ref, *refs):
    pieces, (weight_ref, tokens, sums, sems) = refs[:-4], refs[-4:]
    copies = []
    for i, piece in enumerate(pieces):
        for j in range(BLOCKS):
            n = i * BLOCKS + j
            copies.append(pltpu.make_async_copy(
                piece.at[pl.ds(j * live, live)],
                tokens.at[pl.ds(pl.multiple_of(where_ref[n] * live, live), live)],
                sems.at[n]))
    for copy in copies:
        copy.start()
    for copy in copies:
        copy.wait()
    features = weight_ref.shape[0]
    lanes = 128
    left = lax.broadcasted_iota(jnp.int32, (packed, lanes), 1) < lanes // 2
    for first in range(0, NEAR, 2):
        result = lax.dot_general(
            weight_ref[...], tokens[first * lanes:(first + 2) * lanes],
            (((1,), (1,)), ((), ())), preferred_element_type=jnp.float32)
        for j in range(2):
            here = result[:, j * lanes:(j + 1) * lanes]
            turned = pltpu.roll(here, lanes // 2, 1)
            sums[first + j] = jnp.where(left, here[:packed], turned[features - packed:])
            sums[NEAR + first + j] = jnp.where(left, turned[:packed], here[features - packed:])


def partials(pieces, where, weight, live, packed):
    features, hidden = weight.shape
    rows = BLOCKS * len(pieces) * live
    return pl.pallas_call(
        functools.partial(partial_kernel, live, packed),
        out_shape=[
            jax.ShapeDtypeStruct((rows, hidden), jnp.bfloat16),
            jax.ShapeDtypeStruct((FAR * NEAR, packed, 128), jnp.float32),
        ],
        in_specs=[pl.BlockSpec(memory_space=pltpu.SMEM)] + [pl.BlockSpec(memory_space=pl.ANY)] * len(pieces) + [VMEM],
        out_specs=[VMEM] * 2,
        scratch_shapes=[pltpu.SemaphoreType.DMA((BLOCKS * len(pieces),))],
        compiler_params=pltpu.CompilerParams(vmem_limit_bytes=40 << 20),
        cost_estimate=pl.CostEstimate(
            flops=2 * rows * hidden * features, bytes_accessed=4 * rows * hidden, transcendentals=0),
    )(where, *pieces, weight)


def weight_grad_kernel(inputs, *refs):
    tokens, (out, held) = refs[:-2], refs[-2:]
    features, hidden = out.shape
    width = inputs.shape[2]
    rows = NEAR * width
    for k in range(len(tokens)):
        for y in range(NEAR):
            first = k * rows + y * width
            held[:, first:first + width] = inputs[y, k * features:(k + 1) * features, :]
    for first in range(0, hidden, 256):
        last = min(first + 256, hidden)
        total = None
        for k in range(len(tokens)):
            part = lax.dot_general(
                held[:, k * rows:(k + 1) * rows], tokens[k][:, first:last],
                (((1,), (0,)), ((), ())), preferred_element_type=jnp.float32)
            total = part if total is None else total + part
        out[:, first:last] = total.astype(out.dtype)


def weight_grad(inputs, tokens):
    chunks = len(tokens)
    features = inputs.shape[1] // chunks
    rows, hidden = tokens[0].shape
    return pl.pallas_call(
        weight_grad_kernel,
        out_shape=jax.ShapeDtypeStruct((features, hidden), jnp.bfloat16),
        in_specs=[VMEM] * (1 + chunks),
        out_specs=VMEM,
        scratch_shapes=[pltpu.VMEM((features, chunks * rows), jnp.bfloat16)],
        compiler_params=pltpu.CompilerParams(vmem_limit_bytes=40 << 20),
        cost_estimate=pl.CostEstimate(
            flops=2 * chunks * rows * hidden * features, bytes_accessed=2 * chunks * rows * hidden, transcendentals=0),
    )(inputs, *tokens)


def add_kernel(first_ref, second_ref, out):
    features, lanes = out.shape
    parts = []
    for ref in (first_ref, second_ref):
        total = ref[0]
        for i in range(1, FAR * NEAR):
            total = total + ref[i]
        packed = total.shape[0]
        turned = pltpu.roll(total, lanes // 2, 1)
        parts.append(jnp.concatenate([total[:features - packed], turned], 0))
    first, second = parts
    lane = lax.broadcasted_iota(jnp.int32, (features, lanes), 1)
    quarter = lanes // 4
    result = jnp.where(
        lane < quarter, first,
        jnp.where(lane < 2 * quarter, pltpu.roll(second, quarter, 1),
                  jnp.where(lane < 3 * quarter, pltpu.roll(first, quarter, 1), pltpu.roll(second, 2 * quarter, 1))))
    out[...] = result.astype(out.dtype)


def add_up(received, features):
    return pl.pallas_call(
        add_kernel,
        out_shape=jax.ShapeDtypeStruct((features, 128), jnp.bfloat16),
        in_specs=[VMEM] * 2,
        out_specs=VMEM,
        compiler_params=pltpu.CompilerParams(vmem_limit_bytes=40 << 20),
    )(*received)


def on_device(activations, upstream, weight, bin_fill):
    bin_len, hidden = upstream.shape
    features = activations.shape[1]
    live = bin_len // CHUNKS
    packed = (features // 2 + 7) // 8 * 8
    x, core, row, far = (lax.axis_index(name) for name in ("x", "core", "row", "far"))

    slot_index = jnp.arange(bin_len, dtype=jnp.int32)
    masked = jnp.where((slot_index < bin_fill[0])[:, None], upstream, jnp.zeros_like(upstream))

    mine = activations.T.reshape(features, 2, CHUNKS, live)
    mine = mine.transpose(2, 0, 1, 3).reshape(CHUNKS * features, 2 * live)
    other = lax.ppermute(mine, "far", flips(FAR, 1))
    mine = jnp.where(far == 0, jnp.concatenate([mine, other], 1), jnp.concatenate([other, mine], 1))
    inputs = lax.all_to_all(jnp.broadcast_to(mine, (NEAR,) + mine.shape), "near", 0, 0)

    def place(x_of, core_of, row_of):
        near_of = (x_of % 2 * 2 + core_of) * 2 + row_of // 2
        return (near_of * 2 + x_of // 2) * 2 + row_of % 2

    tokens, received = [], []
    for k in range(CHUNKS):
        block = masked[k * live:(k + 1) * live]
        line = lax.all_to_all(jnp.broadcast_to(block, (ROWS,) + block.shape), "row", 0, 0)
        low, high = (line[:2].reshape(2 * live, hidden), line[2:].reshape(2 * live, hidden))
        low = jnp.concatenate([low, lax.ppermute(low, "x", flips(X, 1))], 0)
        high = jnp.concatenate([high, lax.ppermute(high, "x", flips(X, 3))], 0)
        own = [low, high, lax.ppermute(low, "x", flips(X, 3)), lax.ppermute(high, "x", flips(X, 1))]
        pieces = own + [lax.ppermute(piece, "core", flips(CORES, 1)) for piece in own]
        where = []
        for core_of in (core, 1 - core):
            for x_pair, rows in (((x, x ^ 1), (0, 1)), ((x, x ^ 3), (2, 3)), ((x ^ 3, x ^ 2), (0, 1)), ((x ^ 1, x ^ 2), (2, 3))):
                where += [place(x_of, core_of, row_of) for x_of in x_pair for row_of in rows]
        held, sums = partials(pieces, jnp.stack(where).astype(jnp.int32), weight, live, packed)
        tokens.append(held)
        received.append(lax.all_to_all(sums, ("far", "near"), 0, 0))
    d_weight = weight_grad(inputs, tokens)
    return add_up(received, features).T, d_weight


def solution(mesh):
    fine = Mesh(mesh.devices.reshape(X, CORES, ROWS, FAR, NEAR), ("x", "core", "row", "far", "near"))
    tall, wide = ("x", "core", "row"), ("far", "near")
    return jax.shard_map(
        on_device, mesh=fine,
        in_specs=(P(wide, tall), P(tall, wide), P(tall, wide), P(tall)),
        out_specs=(P(wide, tall), P(tall, wide)), check_vma=False,
    )
```

```python
import functools

import jax
import jax.numpy as jnp
from jax import lax
from jax.experimental import pallas as pl
from jax.experimental.pallas import tpu as pltpu
from jax.sharding import Mesh
from jax.sharding import PartitionSpec as P

CHUNKS = 2
X, CORES, ROWS, FAR, NEAR = 4, 2, 4, 2, 8
BINS = X * CORES * ROWS
OWNERS = FAR * NEAR
VMEM = pl.BlockSpec(memory_space=pltpu.VMEM)
ANY = pl.BlockSpec(memory_space=pl.ANY)
TINY = 2.0 ** -100
SHIFT = 7.5
PARAMS = pltpu.CompilerParams(vmem_limit_bytes=60 << 20)
SMALL = pltpu.CompilerParams(vmem_limit_bytes=16 << 20)


def flips(size, flip):
    return [(i, i ^ flip) for i in range(size)]


def partial_kernel(live, chunk, counts, where_ref, *refs):
    pieces = refs[:len(counts)]
    own_ref, other_ref, tokens_out, sums_out, tokens, sums, in_sems, out_sems = refs[-8:]
    copies = []
    for piece, (first, blocks) in zip(pieces, counts):
        for j in range(blocks):
            n = len(copies)
            copies.append(pltpu.make_async_copy(
                piece.at[pl.ds(first + j * live, live)], tokens.at[where_ref[n]], in_sems.at[n]))
    for copy in copies:
        copy.start()
    for copy in copies:
        copy.wait()
    save = pltpu.make_async_copy(tokens, tokens_out, out_sems.at[0])
    save.start()
    features = own_ref.shape[0]
    rows, lanes = BINS * live, sums.shape[-1]
    lane = lax.broadcasted_iota(jnp.int32, (rows, lanes), 1)
    for i, ref in enumerate((own_ref, other_ref)):
        result = lax.dot_general(
            tokens[...].reshape(rows, ref.shape[1]), ref[...],
            (((1,), (1,)), ((), ())), preferred_element_type=jnp.float32)
        top = jnp.max(jnp.abs(result), axis=1, keepdims=True)
        power = jnp.ceil(jnp.log2(jnp.maximum(top, TINY)))
        raised = result * jnp.exp2(SHIFT - power)
        for _ in range(4):
            raised = raised * raised
        result = jnp.where(result < 0, -raised, raised)
        result = jnp.concatenate([result, jnp.zeros((rows, lanes - features), jnp.float32)], 1)
        coded = jnp.where(lane < features, result, power).astype(sums.dtype)
        sums[:, i] = coded.reshape(OWNERS, 2 * live, lanes)
    send = pltpu.make_async_copy(sums, sums_out.at[:, chunk], out_sems.at[1])
    send.start()
    save.wait()
    send.wait()


def partials(pieces, counts, where, own, other, live, chunk, after, earlier):
    features, hidden = own.shape
    rows = BINS * live
    lanes = features // 128 * 128 + 128
    coded = jax.ShapeDtypeStruct((OWNERS, CHUNKS, 2, 2 * live, lanes), jnp.bfloat16)
    tokens = jax.ShapeDtypeStruct((BINS, live, hidden), jnp.bfloat16)
    after = after + ([] if earlier is None else [earlier])
    return pl.pallas_call(
        functools.partial(partial_kernel, live, chunk, counts),
        out_shape=[tokens, coded],
        in_specs=[pl.BlockSpec(memory_space=pltpu.SMEM)] + [ANY] * (len(pieces) + len(after)) + [VMEM] * 2,
        out_specs=[ANY] * 2,
        input_output_aliases={} if earlier is None else {len(pieces) + len(after): 1},
        scratch_shapes=[
            pltpu.VMEM(tokens.shape, tokens.dtype),
            pltpu.VMEM((OWNERS, 2, 2 * live, lanes), coded.dtype),
            pltpu.SemaphoreType.DMA((BINS,)), pltpu.SemaphoreType.DMA((2,))],
        compiler_params=PARAMS,
        cost_estimate=pl.CostEstimate(
            flops=4 * rows * hidden * features, bytes_accessed=4 * rows * hidden, transcendentals=0),
    )(where, *pieces, *after, own, other)


def weight_grad_kernel(core_ref, inputs, more, *refs):
    parts, (out, held, tokens, sems) = refs[:-4], refs[-4:]
    core = core_ref[0]
    chunks = len(parts) // 2
    copies = []
    for n, part in enumerate(parts):
        half = core if n < chunks else 1 - core
        copies.append(pltpu.make_async_copy(part, tokens.at[:, half * chunks + n % chunks], sems.at[n]))
    for copy in copies:
        copy.start()
    features, hidden = out.shape
    width = inputs.shape[2]
    owner = core_ref[1]
    for i in range(OWNERS):
        flip = (i & 1) * NEAR + (i >> 1 & 1) * 4 + (i >> 2 & 1) * 2 + (i >> 3)
        first = pl.multiple_of((owner ^ flip) * width, width)
        held[:, pl.ds(first, width)] = inputs[i] if i < NEAR else more[i - NEAR]
    for copy in copies:
        copy.wait()
    for first in range(0, hidden, 256):
        last = min(first + 256, hidden)
        rows = tokens[:, :, :, first:last].reshape(held.shape[1], last - first)
        out[:, first:last] = lax.dot_general(
            held[...], rows, (((1,), (0,)), ((), ())), preferred_element_type=jnp.float32).astype(out.dtype)


def weight_grad(core, inputs, parts, live, features):
    hidden = parts[0].shape[2]
    width = inputs[0].shape[2]
    rows = BINS * live * len(parts)
    return pl.pallas_call(
        weight_grad_kernel,
        out_shape=jax.ShapeDtypeStruct((features, hidden), jnp.bfloat16),
        in_specs=[pl.BlockSpec(memory_space=pltpu.SMEM), VMEM, VMEM] + [ANY] * len(parts),
        out_specs=VMEM,
        scratch_shapes=[
            pltpu.VMEM((features, OWNERS * width), jnp.bfloat16),
            pltpu.VMEM((BINS, len(parts), live, hidden), jnp.bfloat16),
            pltpu.SemaphoreType.DMA((len(parts),))],
        compiler_params=PARAMS,
        cost_estimate=pl.CostEstimate(
            flops=2 * rows * hidden * features, bytes_accessed=2 * rows * hidden, transcendentals=0),
    )(core, *inputs, *parts)


def add_kernel(received, after, keep, send):
    del after
    features = keep.shape[1]
    live = received.shape[3] // 2
    for k in range(CHUNKS):
        for i, out in enumerate((keep, send)):
            total = None
            for n in range(OWNERS):
                coded = received[n, k, i].astype(jnp.float32)
                power = coded[:, features:features + 1] - SHIFT
                value = jnp.exp2(jnp.log2(jnp.abs(coded)) * 0.0625 + power)
                value = jnp.where(coded > 0, value, jnp.where(coded < 0, -value, 0.0))
                total = value if total is None else total + value
            for slot in range(2):
                first = (slot * CHUNKS + k) * live
                out[first:first + live] = total[slot * live:(slot + 1) * live, :features]


def add_up(received, features, after):
    rows = CHUNKS * received.shape[3]
    return pl.pallas_call(
        add_kernel,
        out_shape=[jax.ShapeDtypeStruct((rows, features), jnp.float32)] * 2,
        in_specs=[VMEM, ANY],
        out_specs=[VMEM] * 2,
        compiler_params=SMALL,
    )(received, after)


def merge_kernel(core_ref, mine, theirs, out, whole):
    half, features = mine.shape[0] // 2, mine.shape[1]
    for slot in range(2):
        for ref, part in ((mine, core_ref[0]), (theirs, 1 - core_ref[0])):
            first = pl.multiple_of((slot * 2 + part) * half, half)
            whole[pl.ds(first, half), :features] = ref[slot * half:(slot + 1) * half]
    out[...] = whole[...].T[:features].astype(out.dtype)


def merge(core, mine, theirs):
    rows, features = mine.shape
    return pl.pallas_call(
        merge_kernel,
        out_shape=jax.ShapeDtypeStruct((features, 2 * rows), jnp.bfloat16),
        in_specs=[pl.BlockSpec(memory_space=pltpu.SMEM), VMEM, VMEM],
        out_specs=VMEM,
        scratch_shapes=[pltpu.VMEM((2 * rows, (features + 127) // 128 * 128), jnp.float32)],
        compiler_params=SMALL,
    )(core, mine, theirs)


def on_device(activations, upstream, weight, bin_fill):
    bin_len, hidden = upstream.shape
    features = activations.shape[1]
    live = bin_len // (CORES * CHUNKS)
    x, core = lax.axis_index("x"), lax.axis_index("core")
    core_of = core.reshape(1).astype(jnp.int32)

    inputs = activations.T[None]
    inputs = jnp.concatenate([inputs, lax.ppermute(inputs, "far", flips(FAR, 1))], 0)
    other_weight = lax.ppermute(weight, "core", flips(CORES, 1))

    slot_index = jnp.arange(bin_len, dtype=jnp.int32)
    masked = jnp.where((slot_index < bin_fill[0])[:, None], upstream, jnp.zeros_like(upstream))
    both = lax.all_gather(masked, "core", axis=0)
    both, inputs = lax.optimization_barrier((both, inputs))
    both = lax.dynamic_slice_in_dim(both, core * CHUNKS * live, CHUNKS * live, 1)

    def over_x(array, flip):
        return lax.ppermute(array, "x", flips(X, flip))

    def over_row(block):
        block = block.reshape(-1, live, hidden)
        every = jnp.broadcast_to(block[None], (ROWS,) + block.shape)
        return lax.all_to_all(every, "row", 0, 0).reshape(-1, hidden)

    def run(chunk, pieces, after, earlier):
        counts, where = [], []
        for array, places in pieces:
            counts.append((0, len(places)))
            where += [(x_of * CORES + c) * ROWS + r for x_of, r, c in places]
        return partials(
            [array for array, _ in pieces], counts, jnp.stack(where).astype(jnp.int32),
            weight, other_weight, live, chunk, after, earlier)

    def wider(inputs, flip):
        return jnp.concatenate([inputs, lax.ppermute(inputs, "near", flips(NEAR, flip))], 0)

    x_1, x_2, x_3 = x ^ 1, x ^ 2, x ^ 3
    line = over_row(both[:, :live].reshape(CORES * live, hidden))
    first, second = both[0, live:], both[1, live:]
    first = jnp.concatenate([first, over_x(first, 1)], 0)
    second = jnp.concatenate([second, over_x(second, 3)], 0)
    first, second, inputs = lax.optimization_barrier((first, second, inputs))
    columns = jnp.concatenate([first, over_x(first, 3), second, over_x(second, 1)], 0)
    inputs = wider(inputs, 4)
    half = line.shape[0] // 2
    low, high = line[:half], line[half:]
    low = jnp.concatenate([low, over_x(low, 1)], 0)
    high = jnp.concatenate([high, over_x(high, 3)], 0)
    low, high, inputs = lax.optimization_barrier((low, high, inputs))
    row_first = low, over_x(low, 3), high, over_x(high, 1)
    inputs = wider(inputs, 2)
    plane = over_row(columns)
    inputs = [inputs, lax.ppermute(inputs, "near", flips(NEAR, 1))]

    held_0, coded = run(0, [
        (piece, [(x_of, r, c) for x_of in x_pair for r in rows for c in range(CORES)])
        for piece, x_pair, rows in zip(
            row_first, ((x, x_1), (x_3, x_2), (x, x_3), (x_1, x_2)), ((0, 1), (0, 1), (2, 3), (2, 3)))], [], None)
    order = [(x_of, 0) for x_of in (x, x_1, x_3, x_2)] + [(x_of, 1) for x_of in (x, x_3, x_1, x_2)]
    held_1, coded = run(1, [(plane, [(x_of, r, c) for r in range(ROWS) for x_of, c in order])], inputs[1:], coded)
    received = lax.all_to_all(coded, ("far", "near"), 0, 0)

    exchanged = [lax.ppermute(t, "core", flips(CORES, 1)) for t in (held_0, held_1)]
    place = lax.axis_index("far") * NEAR + lax.axis_index("near")
    d_weight = weight_grad(jnp.stack([core, place]).astype(jnp.int32), inputs, [held_0, held_1] + exchanged, live, features)

    keep, send = add_up(received, features, d_weight)
    d_input = merge(core_of, keep, lax.ppermute(send, "core", flips(CORES, 1)))
    return d_input.T, d_weight


def solution(mesh):
    fine = Mesh(mesh.devices.reshape(X, CORES, ROWS, FAR, NEAR), ("x", "core", "row", "far", "near"))
    tall, wide = ("x", "core", "row"), ("far", "near")
    return jax.shard_map(
        on_device, mesh=fine,
        in_specs=(P(wide, tall), P(tall, wide), P(tall, wide), P(tall)),
        out_specs=(P(wide, tall), P(tall, wide)), check_vma=False,
    )
```

```python
import jax
import jax.numpy as jnp
from jax import lax
from jax.experimental import pallas as pl
from jax.experimental.pallas import tpu as pltpu
from jax.sharding import Mesh
from jax.sharding import PartitionSpec as P

X, CORES, ROWS, FAR, NEAR = 4, 2, 4, 2, 8
BINS = X * CORES * ROWS
OWNERS = FAR * NEAR
VMEM = pl.BlockSpec(memory_space=pltpu.VMEM)
SMEM = pl.BlockSpec(memory_space=pltpu.SMEM)
ANY = pl.BlockSpec(memory_space=pl.ANY)
TINY = 2.0 ** -100
SHIFT = 7.5
LARGE = pltpu.CompilerParams(vmem_limit_bytes=60 << 20)
SMALL = pltpu.CompilerParams(vmem_limit_bytes=16 << 20)


def flips(size, flip):
    return [(i, i ^ flip) for i in range(size)]


def coded_of(result, lanes):
    rows, features = result.shape
    top = jnp.max(jnp.abs(result), axis=1, keepdims=True)
    power = jnp.ceil(jnp.log2(jnp.maximum(top, TINY)))
    raised = result * jnp.exp2(SHIFT - power)
    for _ in range(4):
        raised = raised * raised
    result = jnp.where(result < 0, -raised, raised)
    result = jnp.concatenate([result, jnp.zeros((rows, lanes - features), jnp.float32)], 1)
    lane = lax.broadcasted_iota(jnp.int32, (rows, lanes), 1)
    return jnp.where(lane < features, result, power).astype(jnp.bfloat16)


def partial_kernel(count, where_ref, *refs):
    pieces = refs[:count]
    own_ref, other_ref, out, sums, sems = refs[-5:]
    lanes = sums.shape[-1]
    copies = []
    for n, piece in enumerate(pieces):
        live, hidden = piece.shape[2:]
        tokens = piece[...].reshape(8 * live, hidden)
        for i, ref in enumerate((own_ref, other_ref)):
            coded = coded_of(lax.dot_general(
                tokens, ref[...], (((1,), (1,)), ((), ())), preferred_element_type=jnp.float32), lanes)
            for m in range(8):
                owner, slot = n * 4 + m // 4 * 2 + m % 2, m // 2 % 2
                sums[owner, i, slot * live:(slot + 1) * live] = coded[m * live:(m + 1) * live]
        for owner in range(n * 4, n * 4 + 4):
            copies.append(pltpu.make_async_copy(sums.at[owner], out.at[where_ref[owner]], sems.at[owner]))
            copies[-1].start()
    for copy in copies:
        copy.wait()


def partials(pieces, where, own, other, after, earlier):
    features, hidden = own.shape
    rows = sum(piece.size // hidden for piece in pieces)
    lanes = features // 128 * 128 + 128
    coded = jax.ShapeDtypeStruct((OWNERS, 2, rows // (4 * len(pieces)), lanes), jnp.bfloat16)
    after = after + ([] if earlier is None else [earlier])
    return pl.pallas_call(
        lambda *refs: partial_kernel(len(pieces), *refs),
        out_shape=coded,
        in_specs=[SMEM] + [VMEM] * len(pieces) + [ANY] * len(after) + [VMEM] * 2,
        out_specs=ANY,
        input_output_aliases={} if earlier is None else {len(pieces) + len(after): 0},
        scratch_shapes=[
            pltpu.VMEM((4 * len(pieces),) + coded.shape[1:], coded.dtype),
            pltpu.SemaphoreType.DMA((4 * len(pieces),))],
        compiler_params=LARGE,
        cost_estimate=pl.CostEstimate(
            flops=4 * rows * hidden * features, bytes_accessed=2 * rows * hidden, transcendentals=0),
    )(where, *pieces, *after, own, other)


def weight_grad_kernel(place_ref, where_ref, inputs, more, *refs):
    pieces, (out, held, tokens, sems) = refs[:-4], refs[-4:]
    core, owner = place_ref[0], place_ref[1]
    features, hidden = out.shape
    half = len(pieces) // 2
    copies = []
    for n, piece in enumerate(pieces):
        for m in range(8):
            copies.append(pltpu.make_async_copy(
                piece.at[m // 2, m % 2],
                tokens.at[where_ref[n % half * 8 + m], core if n < half else 1 - core],
                sems.at[len(copies)]))
    for copy in copies:
        copy.start()
    width = inputs.shape[2]
    for i in range(OWNERS):
        flip = (i & 1) * 4 + (i & 2) + (i >> 2 & 1) * NEAR + (i >> 3)
        first = pl.multiple_of((owner ^ flip) * width, width)
        held[:, pl.ds(first, width)] = inputs[i] if i < NEAR else more[i - NEAR]
    for copy in copies:
        copy.wait()
    for first in range(0, hidden, 256):
        last = min(first + 256, hidden)
        rows = tokens[:, :, :, first:last].reshape(held.shape[1], last - first)
        out[:, first:last] = lax.dot_general(
            held[...], rows, (((1,), (0,)), ((), ())), preferred_element_type=jnp.float32).astype(out.dtype)


def weight_grad(place, where, inputs, pieces):
    features, width = inputs[0].shape[1:]
    rows, hidden = OWNERS * width, pieces[0].shape[3]
    return pl.pallas_call(
        weight_grad_kernel,
        out_shape=jax.ShapeDtypeStruct((features, hidden), jnp.bfloat16),
        in_specs=[SMEM, SMEM, VMEM, VMEM] + [ANY] * len(pieces),
        out_specs=VMEM,
        scratch_shapes=[
            pltpu.VMEM((features, rows), jnp.bfloat16),
            pltpu.VMEM((BINS, CORES, rows // (BINS * CORES), hidden), jnp.bfloat16),
            pltpu.SemaphoreType.DMA((8 * len(pieces),))],
        compiler_params=LARGE,
        cost_estimate=pl.CostEstimate(
            flops=2 * rows * hidden * features, bytes_accessed=2 * rows * hidden, transcendentals=0),
    )(place, where, *inputs, *pieces)


def add_kernel(received, after, keep, send):
    del after
    features = keep.shape[1]
    for i, out in enumerate((keep, send)):
        total = None
        for n in range(OWNERS):
            coded = received[n, i].astype(jnp.float32)
            power = coded[:, features:features + 1] - SHIFT
            value = jnp.exp2(jnp.log2(jnp.abs(coded)) * 0.0625 + power)
            value = jnp.where(coded > 0, value, jnp.where(coded < 0, -value, 0.0))
            total = value if total is None else total + value
        out[...] = total[:, :features]


def add_up(received, features, after):
    return pl.pallas_call(
        add_kernel,
        out_shape=[jax.ShapeDtypeStruct((received.shape[2], features), jnp.float32)] * 2,
        in_specs=[VMEM, ANY],
        out_specs=[VMEM] * 2,
        compiler_params=SMALL,
    )(received, after)


def merge_kernel(place_ref, mine, theirs, out, whole):
    half, features = mine.shape[0] // 2, mine.shape[1]
    for slot in range(2):
        for ref, part in ((mine, place_ref[0]), (theirs, 1 - place_ref[0])):
            first = pl.multiple_of((slot * 2 + part) * half, half)
            whole[pl.ds(first, half), :features] = ref[slot * half:(slot + 1) * half]
    out[...] = whole[...].T[:features].astype(out.dtype)


def merge(place, mine, theirs):
    rows, features = mine.shape
    return pl.pallas_call(
        merge_kernel,
        out_shape=jax.ShapeDtypeStruct((features, 2 * rows), jnp.bfloat16),
        in_specs=[SMEM, VMEM, VMEM],
        out_specs=VMEM,
        scratch_shapes=[pltpu.VMEM((2 * rows, (features + 127) // 128 * 128), jnp.float32)],
        compiler_params=SMALL,
    )(place, mine, theirs)


def on_device(activations, upstream, weight, bin_fill):
    bin_len, hidden = upstream.shape
    features = activations.shape[1]
    live = bin_len // CORES
    x, core = lax.axis_index("x"), lax.axis_index("core")
    place = jnp.stack([core, lax.axis_index("far") * NEAR + lax.axis_index("near")]).astype(jnp.int32)

    def swap(array):
        return lax.ppermute(array, "core", flips(CORES, 1))

    def over_x(array, flip):
        return lax.ppermute(array, "x", flips(X, flip))

    def wider(inputs, axis, size, flip):
        return jnp.concatenate([inputs, lax.ppermute(inputs, axis, flips(size, flip))], 0)

    slot_index = jnp.arange(bin_len, dtype=jnp.int32)
    masked = jnp.where((slot_index < bin_fill[0])[:, None], upstream, jnp.zeros_like(upstream))
    both = lax.all_gather(masked, "core", axis=0)
    both = lax.dynamic_slice_in_dim(both, core * live, live, 1)
    both, inputs = lax.optimization_barrier((both, activations.T[None]))
    line = lax.all_to_all(jnp.broadcast_to(both[None], (ROWS,) + both.shape), "row", 0, 0)
    inputs = wider(wider(inputs, "near", NEAR, 4), "near", NEAR, 2)
    line, inputs = lax.optimization_barrier((line, inputs))

    other_weight = swap(weight)
    low, high = line[:ROWS // 2], line[ROWS // 2:]
    low = jnp.concatenate([low, over_x(low, 1)], 0)
    high = jnp.concatenate([high, over_x(high, 3)], 0)
    inputs = [wider(inputs, "far", FAR, 1)]
    high, inputs[0] = lax.optimization_barrier((high, inputs[0]))
    far_low, far_high = over_x(low, 3), over_x(high, 1)
    inputs.append(lax.ppermute(inputs[0], "near", flips(NEAR, 1)))

    x_1, x_2, x_3 = x ^ 1, x ^ 2, x ^ 3
    pieces = [low, high, far_low, far_high]
    origins = [((x, x_1), 0), ((x, x_3), 1), ((x_3, x_2), 0), ((x_1, x_2), 1)]
    owners = [(x_of * CORES + c) * 2 + pair for x_pair, pair in origins for x_of in x_pair for c in range(CORES)]
    bins = [(x_of * CORES + c) * ROWS + pair * 2 + r
            for x_pair, pair in origins for x_of in x_pair for r in range(2) for c in range(CORES)]
    owners, bins = (jnp.stack(table).astype(jnp.int32) for table in (owners, bins))

    coded = partials(pieces[:2], owners[:8], weight, other_weight, [], None)
    coded = partials(pieces[2:], owners[8:], weight, other_weight, inputs[1:], coded)
    received = lax.all_to_all(coded, ("far", "near"), 0, 0)
    d_weight = weight_grad(place, bins, inputs, pieces + [swap(piece) for piece in pieces])

    keep, send = add_up(received, features, d_weight)
    d_input = merge(place, keep, swap(send))
    return d_input.T, d_weight


def solution(mesh):
    fine = Mesh(mesh.devices.reshape(X, CORES, ROWS, FAR, NEAR), ("x", "core", "row", "far", "near"))
    tall, wide = ("x", "core", "row"), ("far", "near")
    return jax.shard_map(
        on_device, mesh=fine,
        in_specs=(P(wide, tall), P(tall, wide), P(tall, wide), P(tall)),
        out_specs=(P(wide, tall), P(tall, wide)), check_vma=False,
    )
```

```python
import jax
import jax.numpy as jnp
from jax import lax
from jax.experimental import pallas as pl
from jax.experimental.pallas import tpu as pltpu
from jax.sharding import Mesh
from jax.sharding import PartitionSpec as P

X, CORES, ROWS, FAR, NEAR = 4, 2, 4, 2, 8
BINS = X * CORES * ROWS
OWNERS = FAR * NEAR
VMEM = pl.BlockSpec(memory_space=pltpu.VMEM)
SMEM = pl.BlockSpec(memory_space=pltpu.SMEM)
ANY = pl.BlockSpec(memory_space=pl.ANY)
TINY = 2.0 ** -100
SHIFT = 7.5
LARGE = pltpu.CompilerParams(vmem_limit_bytes=60 << 20)
SMALL = pltpu.CompilerParams(vmem_limit_bytes=16 << 20)


def flips(size, flip):
    return [(i, i ^ flip) for i in range(size)]


def coded_of(result, lanes):
    rows, features = result.shape
    top = jnp.max(jnp.abs(result), axis=1, keepdims=True)
    power = jnp.ceil(jnp.log2(jnp.maximum(top, TINY)))
    raised = result * jnp.exp2(SHIFT - power)
    for _ in range(4):
        raised = raised * raised
    result = jnp.where(result < 0, -raised, raised)
    result = jnp.concatenate([result, jnp.zeros((rows, lanes - features), jnp.float32)], 1)
    lane = lax.broadcasted_iota(jnp.int32, (rows, lanes), 1)
    return jnp.where(lane < features, result, power).astype(jnp.bfloat16)


def partial_kernel(count, where_ref, *refs):
    pieces = refs[:count]
    own_ref, other_ref, out, sums, sems = refs[-5:]
    lanes = sums.shape[-1]
    copies = []
    for n, piece in enumerate(pieces):
        live, hidden = piece.shape[2:]
        tokens = piece[...].reshape(8 * live, hidden)
        for i, ref in enumerate((own_ref, other_ref)):
            coded = coded_of(lax.dot_general(
                tokens, ref[...], (((1,), (1,)), ((), ())), preferred_element_type=jnp.float32), lanes)
            for m in range(8):
                owner, slot = n * 4 + m // 4 * 2 + m % 2, m // 2 % 2
                sums[owner, i, slot * live:(slot + 1) * live] = coded[m * live:(m + 1) * live]
        for owner in range(n * 4, n * 4 + 4):
            for u in range(2):
                slot = pl.multiple_of((where_ref[4 * count] ^ u) * live, live)
                copies.append(pltpu.make_async_copy(
                    sums.at[owner, :, pl.ds(u * live, live)],
                    out.at[where_ref[owner], :, pl.ds(slot, live)], sems.at[len(copies)]))
                copies[-1].start()
    for copy in copies:
        copy.wait()


def partials(pieces, where, own, other, after, earlier):
    features, hidden = own.shape
    rows = sum(piece.size // hidden for piece in pieces)
    lanes = features // 128 * 128 + 128
    coded = jax.ShapeDtypeStruct((OWNERS, 2, rows // (4 * len(pieces)), lanes), jnp.bfloat16)
    after = after + ([] if earlier is None else [earlier])
    return pl.pallas_call(
        lambda *refs: partial_kernel(len(pieces), *refs),
        out_shape=coded,
        in_specs=[SMEM] + [VMEM] * len(pieces) + [ANY] * len(after) + [VMEM] * 2,
        out_specs=ANY,
        input_output_aliases={} if earlier is None else {len(pieces) + len(after): 0},
        scratch_shapes=[
            pltpu.VMEM((4 * len(pieces),) + coded.shape[1:], coded.dtype),
            pltpu.SemaphoreType.DMA((8 * len(pieces),))],
        compiler_params=LARGE,
        cost_estimate=pl.CostEstimate(
            flops=4 * rows * hidden * features, bytes_accessed=2 * rows * hidden, transcendentals=0),
    )(where, *pieces, *after, own, other)


def weight_grad_kernel(place_ref, where_ref, inputs, more, *refs):
    pieces, (out, held, tokens, sems) = refs[:-4], refs[-4:]
    core, owner = place_ref[0], place_ref[1]
    features, hidden = out.shape
    half = len(pieces) // 2
    copies = []
    for n, piece in enumerate(pieces):
        for m in range(8):
            copies.append(pltpu.make_async_copy(
                piece.at[m // 2, m % 2],
                tokens.at[where_ref[n % half * 8 + m], core if n < half else 1 - core],
                sems.at[len(copies)]))
    for copy in copies:
        copy.start()
    width = inputs.shape[2]
    for i in range(OWNERS):
        flip = (i & 1) * 4 + (i & 2) + (i >> 2 & 1) * NEAR + (i >> 3)
        first = pl.multiple_of((owner ^ flip) * width, width)
        held[:, pl.ds(first, width)] = inputs[i] if i < NEAR else more[i - NEAR]
    for copy in copies:
        copy.wait()
    for first in range(0, hidden, 256):
        last = min(first + 256, hidden)
        rows = tokens[:, :, :, first:last].reshape(held.shape[1], last - first)
        out[:, first:last] = lax.dot_general(
            held[...], rows, (((1,), (0,)), ((), ())), preferred_element_type=jnp.float32).astype(out.dtype)


def weight_grad(place, where, inputs, pieces):
    features, width = inputs[0].shape[1:]
    rows, hidden = OWNERS * width, pieces[0].shape[3]
    return pl.pallas_call(
        weight_grad_kernel,
        out_shape=jax.ShapeDtypeStruct((features, hidden), jnp.bfloat16),
        in_specs=[SMEM, SMEM, VMEM, VMEM] + [ANY] * len(pieces),
        out_specs=VMEM,
        scratch_shapes=[
            pltpu.VMEM((features, rows), jnp.bfloat16),
            pltpu.VMEM((BINS, CORES, rows // (BINS * CORES), hidden), jnp.bfloat16),
            pltpu.SemaphoreType.DMA((8 * len(pieces),))],
        compiler_params=LARGE,
        cost_estimate=pl.CostEstimate(
            flops=2 * rows * hidden * features, bytes_accessed=2 * rows * hidden, transcendentals=0),
    )(place, where, *inputs, *pieces)


def add_kernel(received, after, keep, send):
    del after
    features = keep.shape[1]
    for i, out in enumerate((keep, send)):
        total = None
        for n in range(OWNERS):
            coded = received[n, i].astype(jnp.float32)
            power = coded[:, features:features + 1] - SHIFT
            value = jnp.exp2(jnp.log2(jnp.abs(coded)) * 0.0625 + power)
            value = jnp.where(coded > 0, value, jnp.where(coded < 0, -value, 0.0))
            total = value if total is None else total + value
        out[...] = total[:, :features]


def add_up(received, features, after):
    return pl.pallas_call(
        add_kernel,
        out_shape=[jax.ShapeDtypeStruct((received.shape[2], features), jnp.float32)] * 2,
        in_specs=[VMEM, ANY],
        out_specs=[VMEM] * 2,
        compiler_params=SMALL,
    )(received, after)


def merge_kernel(place_ref, mine, theirs, out, whole):
    half, features = mine.shape[0] // 2, mine.shape[1]
    for slot in range(2):
        for ref, part in ((mine, place_ref[0]), (theirs, 1 - place_ref[0])):
            first = pl.multiple_of((slot * 2 + part) * half, half)
            whole[pl.ds(first, half), :features] = ref[slot * half:(slot + 1) * half]
    out[...] = whole[...].T[:features].astype(out.dtype)


def merge(place, mine, theirs):
    rows, features = mine.shape
    return pl.pallas_call(
        merge_kernel,
        out_shape=jax.ShapeDtypeStruct((features, 2 * rows), jnp.bfloat16),
        in_specs=[SMEM, VMEM, VMEM],
        out_specs=VMEM,
        scratch_shapes=[pltpu.VMEM((2 * rows, (features + 127) // 128 * 128), jnp.float32)],
        compiler_params=SMALL,
    )(place, mine, theirs)


def on_device(activations, upstream, weight, bin_fill):
    bin_len, hidden = upstream.shape
    features = activations.shape[1]
    live = bin_len // CORES
    x, core = lax.axis_index("x"), lax.axis_index("core")
    place = jnp.stack([core, lax.axis_index("far") * NEAR + lax.axis_index("near")]).astype(jnp.int32)

    def swap(array):
        return lax.ppermute(array, "core", flips(CORES, 1))

    def over_x(array, flip):
        return lax.ppermute(array, "x", flips(X, flip))

    def wider(inputs, axis, size, flip):
        return jnp.concatenate([inputs, lax.ppermute(inputs, axis, flips(size, flip))], 0)

    slot_index = jnp.arange(bin_len, dtype=jnp.int32)
    masked = jnp.where((slot_index < bin_fill[0])[:, None], upstream, jnp.zeros_like(upstream))
    both = lax.all_gather(masked, "core", axis=0)
    both = lax.dynamic_slice_in_dim(both, core * live, live, 1)
    both, inputs = lax.optimization_barrier((both, activations.T[None]))
    rows = [both] + [lax.ppermute(both, "row", flips(ROWS, flip)) for flip in (1, 2, 3)]
    inputs = wider(wider(inputs, "near", NEAR, 4), "near", NEAR, 2)

    other_weight = swap(weight)
    low, high = jnp.stack(rows[:2]), jnp.stack(rows[2:])
    low = jnp.concatenate([low, over_x(low, 1)], 0)
    high = jnp.concatenate([high, over_x(high, 3)], 0)
    low, inputs = lax.optimization_barrier((low, inputs))
    inputs = [wider(inputs, "far", FAR, 1)]
    high, inputs[0] = lax.optimization_barrier((high, inputs[0]))
    far_low, far_high = over_x(low, 3), over_x(high, 1)
    inputs.append(lax.ppermute(inputs[0], "near", flips(NEAR, 1)))

    x_1, x_2, x_3 = x ^ 1, x ^ 2, x ^ 3
    row = lax.axis_index("row")
    pieces = [low, high, far_low, far_high]
    origins = [((x, x_1), 0), ((x, x_3), 2), ((x_3, x_2), 0), ((x_1, x_2), 2)]
    owners = [(x_of * CORES + c) * 2 + (row ^ flip) // 2
              for x_pair, flip in origins for x_of in x_pair for c in range(CORES)]
    bins = [(x_of * CORES + c) * ROWS + (row ^ flip ^ u)
            for x_pair, flip in origins for x_of in x_pair for u in range(2) for c in range(CORES)]
    tables = [jnp.stack(table).astype(jnp.int32) for table in (owners[:8] + [row % 2], owners[8:] + [row % 2], bins)]

    coded = partials(pieces[:2], tables[0], weight, other_weight, [], None)
    coded = partials(pieces[2:], tables[1], weight, other_weight, inputs[1:], coded)
    received = lax.all_to_all(coded, ("far", "near"), 0, 0)
    d_weight = weight_grad(place, tables[2], inputs, pieces + [swap(piece) for piece in pieces])

    keep, send = add_up(received, features, d_weight)
    d_input = merge(place, keep, swap(send))
    return d_input.T, d_weight


def solution(mesh):
    fine = Mesh(mesh.devices.reshape(X, CORES, ROWS, FAR, NEAR), ("x", "core", "row", "far", "near"))
    tall, wide = ("x", "core", "row"), ("far", "near")
    return jax.shard_map(
        on_device, mesh=fine,
        in_specs=(P(wide, tall), P(tall, wide), P(tall, wide), P(tall)),
        out_specs=(P(wide, tall), P(tall, wide)), check_vma=False,
    )
```

```python
import jax
import jax.numpy as jnp
from jax import lax
from jax.experimental import pallas as pl
from jax.experimental.pallas import tpu as pltpu
from jax.sharding import Mesh
from jax.sharding import PartitionSpec as P

X, CORES, ROWS, FAR, NEAR = 4, 2, 4, 2, 8
BINS = X * CORES * ROWS
OWNERS = FAR * NEAR
VMEM = pl.BlockSpec(memory_space=pltpu.VMEM)
SMEM = pl.BlockSpec(memory_space=pltpu.SMEM)
ANY = pl.BlockSpec(memory_space=pl.ANY)
TINY = 2.0 ** -100
SHIFT = 7.5
LARGE = pltpu.CompilerParams(vmem_limit_bytes=60 << 20)
SMALL = pltpu.CompilerParams(vmem_limit_bytes=16 << 20)


def flips(size, flip):
    return [(i, i ^ flip) for i in range(size)]


def coded_of(result, lanes):
    rows, features = result.shape
    top = jnp.max(jnp.abs(result), axis=1, keepdims=True)
    power = jnp.ceil(jnp.log2(jnp.maximum(top, TINY)))
    raised = result * jnp.exp2(SHIFT - power)
    for _ in range(4):
        raised = raised * raised
    result = jnp.where(result < 0, -raised, raised)
    result = jnp.concatenate([result, jnp.zeros((rows, lanes - features), jnp.float32)], 1)
    lane = lax.broadcasted_iota(jnp.int32, (rows, lanes), 1)
    return jnp.where(lane < features, result, power).astype(jnp.bfloat16)


def partial_kernel(count, where_ref, *refs):
    pieces = refs[:count]
    own_ref, other_ref, out, sums, sems = refs[-5:]
    copies = []
    for n, piece in enumerate(pieces):
        places, cores, live, hidden = piece.shape
        blocks = places * cores
        tokens = piece[...].reshape(blocks * live, hidden)
        for i, ref in enumerate((own_ref, other_ref)):
            coded = coded_of(lax.dot_general(
                tokens, ref[...], (((1,), (1,)), ((), ())), preferred_element_type=jnp.float32), sums.shape[-1])
            for m in range(blocks):
                sums[n * blocks + m, i] = coded[m * live:(m + 1) * live]
        for m in range(n * blocks, (n + 1) * blocks):
            slot = pl.multiple_of(where_ref[m] % 2 * live, live)
            copies.append(pltpu.make_async_copy(
                sums.at[m], out.at[where_ref[m] // 2, :, pl.ds(slot, live)], sems.at[m]))
            copies[-1].start()
    for copy in copies:
        copy.wait()


def partials(pieces, where, own, other, after, earlier):
    features, hidden = own.shape
    rows = sum(piece.size // hidden for piece in pieces)
    lanes = features // 128 * 128 + 128
    coded = jax.ShapeDtypeStruct((OWNERS, 2, rows // (4 * len(pieces)), lanes), jnp.bfloat16)
    after = after + ([] if earlier is None else [earlier])
    return pl.pallas_call(
        lambda *refs: partial_kernel(len(pieces), *refs),
        out_shape=coded,
        in_specs=[SMEM] + [VMEM] * len(pieces) + [ANY] * len(after) + [VMEM] * 2,
        out_specs=ANY,
        input_output_aliases={} if earlier is None else {len(pieces) + len(after): 0},
        scratch_shapes=[
            pltpu.VMEM((8 * len(pieces), 2, coded.shape[2] // 2, lanes), coded.dtype),
            pltpu.SemaphoreType.DMA((8 * len(pieces),))],
        compiler_params=LARGE,
        cost_estimate=pl.CostEstimate(
            flops=4 * rows * hidden * features, bytes_accessed=2 * rows * hidden, transcendentals=0),
    )(where, *pieces, *after, own, other)


def weight_grad_kernel(place_ref, where_ref, inputs, more, *refs):
    pieces, (out, held, tokens, sems) = refs[:-4], refs[-4:]
    core, owner = place_ref[0], place_ref[1]
    features, hidden = out.shape
    half = len(pieces) // 2
    copies = []
    for n, piece in enumerate(pieces):
        for m in range(8):
            copies.append(pltpu.make_async_copy(
                piece.at[m // 2, m % 2],
                tokens.at[where_ref[n % half * 8 + m], core if n < half else 1 - core],
                sems.at[len(copies)]))
    for copy in copies:
        copy.start()
    width = inputs.shape[2]
    for i in range(OWNERS):
        flip = (i & 1) * 4 + (i & 2) + (i >> 2 & 1) * NEAR + (i >> 3)
        first = pl.multiple_of((owner ^ flip) * width, width)
        held[:, pl.ds(first, width)] = inputs[i] if i < NEAR else more[i - NEAR]
    for copy in copies:
        copy.wait()
    for first in range(0, hidden, 256):
        last = min(first + 256, hidden)
        rows = tokens[:, :, :, first:last].reshape(held.shape[1], last - first)
        out[:, first:last] = lax.dot_general(
            held[...], rows, (((1,), (0,)), ((), ())), preferred_element_type=jnp.float32).astype(out.dtype)


def weight_grad(place, where, inputs, pieces):
    features, width = inputs[0].shape[1:]
    rows, hidden = OWNERS * width, pieces[0].shape[3]
    return pl.pallas_call(
        weight_grad_kernel,
        out_shape=jax.ShapeDtypeStruct((features, hidden), jnp.bfloat16),
        in_specs=[SMEM, SMEM, VMEM, VMEM] + [ANY] * len(pieces),
        out_specs=VMEM,
        scratch_shapes=[
            pltpu.VMEM((features, rows), jnp.bfloat16),
            pltpu.VMEM((BINS, CORES, rows // (BINS * CORES), hidden), jnp.bfloat16),
            pltpu.SemaphoreType.DMA((8 * len(pieces),))],
        compiler_params=LARGE,
        cost_estimate=pl.CostEstimate(
            flops=2 * rows * hidden * features, bytes_accessed=2 * rows * hidden, transcendentals=0),
    )(place, where, *inputs, *pieces)


def add_kernel(received, after, keep, send):
    del after
    features = keep.shape[1]
    for i, out in enumerate((keep, send)):
        total = None
        for n in range(OWNERS):
            coded = received[n, i].astype(jnp.float32)
            power = coded[:, features:features + 1] - SHIFT
            value = jnp.exp2(jnp.log2(jnp.abs(coded)) * 0.0625 + power)
            value = jnp.where(coded > 0, value, jnp.where(coded < 0, -value, 0.0))
            total = value if total is None else total + value
        out[...] = total[:, :features]


def add_up(received, features, after):
    return pl.pallas_call(
        add_kernel,
        out_shape=[jax.ShapeDtypeStruct((received.shape[2], features), jnp.float32)] * 2,
        in_specs=[VMEM, ANY],
        out_specs=[VMEM] * 2,
        compiler_params=SMALL,
    )(received, after)


def merge_kernel(place_ref, mine, theirs, out, whole):
    half, features = mine.shape[0] // 2, mine.shape[1]
    for slot in range(2):
        for ref, part in ((mine, place_ref[0]), (theirs, 1 - place_ref[0])):
            first = pl.multiple_of((slot * 2 + part) * half, half)
            whole[pl.ds(first, half), :features] = ref[slot * half:(slot + 1) * half]
    out[...] = whole[...].T[:features].astype(out.dtype)


def merge(place, mine, theirs):
    rows, features = mine.shape
    return pl.pallas_call(
        merge_kernel,
        out_shape=jax.ShapeDtypeStruct((features, 2 * rows), jnp.bfloat16),
        in_specs=[SMEM, VMEM, VMEM],
        out_specs=VMEM,
        scratch_shapes=[pltpu.VMEM((2 * rows, (features + 127) // 128 * 128), jnp.float32)],
        compiler_params=SMALL,
    )(place, mine, theirs)


def on_device(activations, upstream, weight, bin_fill):
    bin_len, hidden = upstream.shape
    features = activations.shape[1]
    live = bin_len // CORES
    x, core = lax.axis_index("x"), lax.axis_index("core")
    place = jnp.stack([core, lax.axis_index("far") * NEAR + lax.axis_index("near")]).astype(jnp.int32)

    def swap(array):
        return lax.ppermute(array, "core", flips(CORES, 1))

    def over_x(array, flip):
        return lax.ppermute(array, "x", flips(X, flip))

    def wider(inputs, axis, size, flip):
        return jnp.concatenate([inputs, lax.ppermute(inputs, axis, flips(size, flip))], 0)

    slot_index = jnp.arange(bin_len, dtype=jnp.int32)
    masked = jnp.where((slot_index < bin_fill[0])[:, None], upstream, jnp.zeros_like(upstream))
    both = lax.all_gather(masked, "core", axis=0)
    both = lax.dynamic_slice_in_dim(both, core * live, live, 1)
    both, inputs = lax.optimization_barrier((both, activations.T[None]))
    rows = [both] + [lax.ppermute(both, "row", flips(ROWS, flip)) for flip in (2, 3, 1)]
    inputs = wider(wider(inputs, "near", NEAR, 4), "near", NEAR, 2)

    other_weight = swap(weight)
    low, high = jnp.stack(rows[:2]), jnp.stack(rows[2:])
    low = jnp.concatenate([low, over_x(low, 1)], 0)
    high = jnp.concatenate([high, over_x(high, 3)], 0)
    low, inputs = lax.optimization_barrier((low, inputs))
    inputs = [wider(inputs, "far", FAR, 1)]
    high, inputs[0] = lax.optimization_barrier((high, inputs[0]))
    far_low, far_high = over_x(low, 3), over_x(high, 1)
    inputs.append(lax.ppermute(inputs[0], "near", flips(NEAR, 1)))

    x_1, x_2, x_3 = x ^ 1, x ^ 2, x ^ 3
    row = lax.axis_index("row")
    pieces = [low, high, far_low, far_high]
    origins = [((x, x_1), (0, 2)), ((x, x_3), (3, 1)), ((x_3, x_2), (0, 2)), ((x_1, x_2), (3, 1))]
    bins = jnp.stack([
        (x_of * CORES + c) * ROWS + (row ^ flip)
        for x_pair, pair in origins for x_of in x_pair for flip in pair for c in range(CORES)]).astype(jnp.int32)

    coded = partials(pieces[:2], bins[:16], weight, other_weight, [], None)
    coded = partials(pieces[2:], bins[16:], weight, other_weight, inputs[1:], coded)
    received = lax.all_to_all(coded, ("far", "near"), 0, 0)
    d_weight = weight_grad(place, bins, inputs, pieces + [swap(piece) for piece in pieces])

    keep, send = add_up(received, features, d_weight)
    d_input = merge(place, keep, swap(send))
    return d_input.T, d_weight


def solution(mesh):
    fine = Mesh(mesh.devices.reshape(X, CORES, ROWS, FAR, NEAR), ("x", "core", "row", "far", "near"))
    tall, wide = ("x", "core", "row"), ("far", "near")
    return jax.shard_map(
        on_device, mesh=fine,
        in_specs=(P(wide, tall), P(tall, wide), P(tall, wide), P(tall)),
        out_specs=(P(wide, tall), P(tall, wide)), check_vma=False,
    )
```

```python
import jax
import jax.numpy as jnp
from jax import lax
from jax.experimental import pallas as pl
from jax.experimental.pallas import tpu as pltpu
from jax.sharding import Mesh
from jax.sharding import PartitionSpec as P

X, CORES, ROWS, FAR, NEAR = 4, 2, 4, 2, 8
BINS = X * CORES * ROWS
OWNERS = FAR * NEAR
VMEM = pl.BlockSpec(memory_space=pltpu.VMEM)
SMEM = pl.BlockSpec(memory_space=pltpu.SMEM)
ANY = pl.BlockSpec(memory_space=pl.ANY)
TINY = 2.0 ** -100
SHIFT = 7.5
LARGE = pltpu.CompilerParams(vmem_limit_bytes=60 << 20)
SMALL = pltpu.CompilerParams(vmem_limit_bytes=16 << 20)


def flips(size, flip):
    return [(i, i ^ flip) for i in range(size)]


def coded_of(result, lanes):
    rows, features = result.shape
    top = jnp.max(jnp.abs(result), axis=1, keepdims=True)
    power = jnp.ceil(jnp.log2(jnp.maximum(top, TINY)))
    raised = result * jnp.exp2(SHIFT - power)
    for _ in range(4):
        raised = raised * raised
    result = jnp.where(result < 0, -raised, raised)
    result = jnp.concatenate([result, jnp.zeros((rows, lanes - features), jnp.float32)], 1)
    lane = lax.broadcasted_iota(jnp.int32, (rows, lanes), 1)
    return jnp.where(lane < features, result, power).astype(jnp.bfloat16)


def partial_kernel(count, where_ref, *refs):
    pieces = refs[:count]
    own_ref, other_ref, out, sums, sems = refs[-5:]
    copies = []
    for n, piece in enumerate(pieces):
        places, cores, live, hidden = piece.shape
        blocks = places * cores
        tokens = piece[...].reshape(blocks * live, hidden)
        for i, ref in enumerate((own_ref, other_ref)):
            coded = coded_of(lax.dot_general(
                tokens, ref[...], (((1,), (1,)), ((), ())), preferred_element_type=jnp.float32), sums.shape[-1])
            for m in range(blocks):
                sums[n * blocks + m, i] = coded[m * live:(m + 1) * live]
        for m in range(n * blocks, (n + 1) * blocks):
            slot = pl.multiple_of(where_ref[m] % 2 * live, live)
            copies.append(pltpu.make_async_copy(
                sums.at[m], out.at[where_ref[m] // 2, :, pl.ds(slot, live)], sems.at[m]))
            copies[-1].start()
    for copy in copies:
        copy.wait()


def partials(pieces, where, own, other, after, earlier):
    features, hidden = own.shape
    rows = sum(piece.size // hidden for piece in pieces)
    lanes = features // 128 * 128 + 128
    coded = jax.ShapeDtypeStruct((OWNERS, 2, rows // (4 * len(pieces)), lanes), jnp.bfloat16)
    after = after + ([] if earlier is None else [earlier])
    return pl.pallas_call(
        lambda *refs: partial_kernel(len(pieces), *refs),
        out_shape=coded,
        in_specs=[SMEM] + [VMEM] * len(pieces) + [ANY] * len(after) + [VMEM] * 2,
        out_specs=ANY,
        input_output_aliases={} if earlier is None else {len(pieces) + len(after): 0},
        scratch_shapes=[
            pltpu.VMEM((8 * len(pieces), 2, coded.shape[2] // 2, lanes), coded.dtype),
            pltpu.SemaphoreType.DMA((8 * len(pieces),))],
        compiler_params=LARGE,
        cost_estimate=pl.CostEstimate(
            flops=4 * rows * hidden * features, bytes_accessed=2 * rows * hidden, transcendentals=0),
    )(where, *pieces, *after, own, other)


def weight_grad_kernel(place_ref, where_ref, inputs, more, *refs):
    pieces, (out, held, tokens, sems) = refs[:-4], refs[-4:]
    core, owner = place_ref[0], place_ref[1]
    features, hidden = out.shape
    half = len(pieces) // 2
    copies = []
    for n, piece in enumerate(pieces):
        for m in range(8):
            copies.append(pltpu.make_async_copy(
                piece.at[m // 2, m % 2],
                tokens.at[where_ref[n % half * 8 + m], core if n < half else 1 - core],
                sems.at[len(copies)]))
    for copy in copies:
        copy.start()
    width = inputs.shape[2]
    for i in range(OWNERS):
        flip = (i & 1) * 4 + (i & 2) + (i >> 2 & 1) * NEAR + (i >> 3)
        first = pl.multiple_of((owner ^ flip) * width, width)
        held[:, pl.ds(first, width)] = inputs[i] if i < NEAR else more[i - NEAR]
    for copy in copies:
        copy.wait()
    for first in range(0, hidden, 256):
        last = min(first + 256, hidden)
        rows = tokens[:, :, :, first:last].reshape(held.shape[1], last - first)
        out[:, first:last] = lax.dot_general(
            held[...], rows, (((1,), (0,)), ((), ())), preferred_element_type=jnp.float32).astype(out.dtype)


def weight_grad(place, where, inputs, pieces):
    features, width = inputs[0].shape[1:]
    rows, hidden = OWNERS * width, pieces[0].shape[3]
    return pl.pallas_call(
        weight_grad_kernel,
        out_shape=jax.ShapeDtypeStruct((features, hidden), jnp.bfloat16),
        in_specs=[SMEM, SMEM, VMEM, VMEM] + [ANY] * len(pieces),
        out_specs=VMEM,
        scratch_shapes=[
            pltpu.VMEM((features, rows), jnp.bfloat16),
            pltpu.VMEM((BINS, CORES, rows // (BINS * CORES), hidden), jnp.bfloat16),
            pltpu.SemaphoreType.DMA((8 * len(pieces),))],
        compiler_params=LARGE,
        cost_estimate=pl.CostEstimate(
            flops=2 * rows * hidden * features, bytes_accessed=2 * rows * hidden, transcendentals=0),
    )(place, where, *inputs, *pieces)


def add_kernel(received, after, keep, send):
    del after
    features = keep.shape[1]
    for i, out in enumerate((keep, send)):
        total = None
        for n in range(OWNERS):
            coded = received[n, i].astype(jnp.float32)
            power = coded[:, features:features + 1] - SHIFT
            value = jnp.exp2(jnp.log2(jnp.abs(coded)) * 0.0625 + power)
            value = jnp.where(coded > 0, value, jnp.where(coded < 0, -value, 0.0))
            total = value if total is None else total + value
        out[...] = total[:, :features]


def add_up(received, features, after):
    return pl.pallas_call(
        add_kernel,
        out_shape=[jax.ShapeDtypeStruct((received.shape[2], features), jnp.float32)] * 2,
        in_specs=[VMEM, ANY],
        out_specs=[VMEM] * 2,
        compiler_params=SMALL,
    )(received, after)


def merge_kernel(place_ref, mine, theirs, out, whole):
    half, features = mine.shape[0] // 2, mine.shape[1]
    for slot in range(2):
        other = 1 - place_ref[0]
        for block, part in (
                (mine[slot * half:(slot + 1) * half], place_ref[0]),
                (theirs[other, slot * half:(slot + 1) * half], other)):
            first = pl.multiple_of((slot * 2 + part) * half, half)
            whole[pl.ds(first, half), :features] = block
    out[...] = whole[...].T[:features].astype(out.dtype)


def merge(place, mine, theirs):
    rows, features = mine.shape
    return pl.pallas_call(
        merge_kernel,
        out_shape=jax.ShapeDtypeStruct((features, 2 * rows), jnp.bfloat16),
        in_specs=[SMEM, VMEM, VMEM],
        out_specs=VMEM,
        scratch_shapes=[pltpu.VMEM((2 * rows, (features + 127) // 128 * 128), jnp.float32)],
        compiler_params=SMALL,
    )(place, mine, theirs)


def on_device(activations, upstream, weight, bin_fill):
    bin_len, hidden = upstream.shape
    features = activations.shape[1]
    live = bin_len // CORES
    x, core = lax.axis_index("x"), lax.axis_index("core")
    place = jnp.stack([core, lax.axis_index("far") * NEAR + lax.axis_index("near")]).astype(jnp.int32)

    def swap(array):
        return lax.ppermute(array, "core", flips(CORES, 1))

    def over_x(array, flip):
        return lax.ppermute(array, "x", flips(X, flip))

    def wider(inputs, axis, size, flip):
        return jnp.concatenate([inputs, lax.ppermute(inputs, axis, flips(size, flip))], 0)

    slot_index = jnp.arange(bin_len, dtype=jnp.int32)
    masked = jnp.where((slot_index < bin_fill[0])[:, None], upstream, jnp.zeros_like(upstream))
    both = lax.all_gather(masked, "core", axis=0)
    both = lax.dynamic_slice_in_dim(both, core * live, live, 1)
    both, inputs = lax.optimization_barrier((both, activations.T[None]))
    rows = [both] + [lax.ppermute(both, "row", flips(ROWS, flip)) for flip in (2, 3, 1)]
    inputs = wider(wider(inputs, "near", NEAR, 4), "near", NEAR, 2)

    other_weight = swap(weight)
    low, high = jnp.stack(rows[:2]), jnp.stack(rows[2:])
    low = jnp.concatenate([low, over_x(low, 1)], 0)
    high = jnp.concatenate([high, over_x(high, 3)], 0)
    low, inputs = lax.optimization_barrier((low, inputs))
    inputs = [wider(inputs, "far", FAR, 1)]
    high, inputs[0] = lax.optimization_barrier((high, inputs[0]))
    far_low, far_high = over_x(low, 3), over_x(high, 1)
    inputs.append(lax.ppermute(inputs[0], "near", flips(NEAR, 1)))

    x_1, x_2, x_3 = x ^ 1, x ^ 2, x ^ 3
    row = lax.axis_index("row")
    pieces = [low, high, far_low, far_high]
    origins = [((x, x_1), (0, 2)), ((x, x_3), (3, 1)), ((x_3, x_2), (0, 2)), ((x_1, x_2), (3, 1))]
    bins = jnp.stack([
        (x_of * CORES + c) * ROWS + (row ^ flip)
        for x_pair, pair in origins for x_of in x_pair for flip in pair for c in range(CORES)]).astype(jnp.int32)

    coded = partials(pieces[:2], bins[:16], weight, other_weight, [], None)
    coded = partials(pieces[2:], bins[16:], weight, other_weight, inputs[1:], coded)
    received = lax.all_to_all(coded, ("far", "near"), 0, 0)
    d_weight = weight_grad(place, bins, inputs, pieces + [swap(piece) for piece in pieces])

    keep, send = add_up(received, features, d_weight)
    d_input = merge(place, keep, lax.all_gather(send, "core", axis=0))
    return d_input.T, d_weight


def solution(mesh):
    fine = Mesh(mesh.devices.reshape(X, CORES, ROWS, FAR, NEAR), ("x", "core", "row", "far", "near"))
    tall, wide = ("x", "core", "row"), ("far", "near")
    return jax.shard_map(
        on_device, mesh=fine,
        in_specs=(P(wide, tall), P(tall, wide), P(tall, wide), P(tall)),
        out_specs=(P(wide, tall), P(tall, wide)), check_vma=False,
    )
```
